32 devices in a mesh: group: 2 (over y), replica: 8 (over z, x), tensor: 2 (over core).
Axes of the slice: x: 2, y: 2, z: 4, core: 2. Of those that a mesh axis runs over, the one named last changes fastest.
Arguments:
- hidden: bfloat16 [1536, 1, 4096], P(('group', 'replica'), None, 'tensor'), parts along dimension 0, may hold values from -6 to 6
- queries: bfloat16 [1536, 1, 4, 1024], P(('group', 'replica'), None, 'tensor'), parts along dimension 0, may hold values from -200 to 200
- incoming_keys: bfloat16 [1536, 1, 4, 128], P(('group', 'replica'), None, 'tensor'), parts along dimension 0, may hold values from -6 to 6
- stored_key_cache: bfloat16 [1536, 4, 16, 128], P(('group', 'replica'), 'tensor'), parts along dimension 0, may hold values from -6 to 6
- stored_value_cache: bfloat16 [1536, 4, 16, 128], P(('group', 'replica'), 'tensor'), parts along dimension 0, may hold values from -6 to 6
- base_value_weight: bfloat16 [4096, 512], P('tensor'), may hold values from -0.09375 to 0.09375
- adapter_down_rows: bfloat16 [8, 64, 4096], P('replica', None, 'tensor'), may hold values from -0.09375 to 0.09375
- adapter_up_rows: bfloat16 [8, 64, 512], P('replica', None, 'tensor'), may hold values from -0.75 to 0.75
- request_adapter: int32 [768], P('replica'), may hold values from 0 to 7, as said below
- adapter_replica: int32 [8], replicated, may hold values from 0 to 7, as said below
- replica_slot_count: int32 [8], P('replica'), may hold values from 84 to 96, as said below
- cache_length: int32 [768], P('replica'), may hold values from 2 to 16, as said below
Outputs:
- attention: bfloat16 [1536, 1, 4, 1024], P(('group', 'replica'), None, 'tensor'), parts along dimension 0
- new_values: bfloat16 [1536, 1, 4, 128], P(('group', 'replica'), None, 'tensor'), parts along dimension 0
The draws below stay inside these ranges and needn't reach their ends.
There are 2 independent parts, one for each index of `group`. The reference program is written for one: setup_inputs(seed, part) draws one part's arguments, and reference() takes and returns one part's arrays. A program takes and returns all parts, laid end to end along the dimension named above; an argument that names none is the same for every part. Nothing has to cross between parts.
Inputs may be any that keep to these rules, and one draw needn't show every extreme that they name: `request_adapter`: among the slots of one replica at most 24 have adapters of one home, and some home has 24 in every replica's first 24 slots. `adapter_replica`: A permutation. `replica_slot_count`: slots 0 to load - 1 of a replica are live; some replica is full. `cache_length`: some slot uses all 16 positions.
All inputs are finite; a program needn't handle non-finite values.
Results may differ from the reference program's by a relative error of at most 0.0053.
Values may be sent and summed in bfloat16 or wider, within the bound.
No kernel may reach another device: no remote copies, remote signals or barrier semaphores. Data moves between devices by JAX's collectives and lax.ppermute only.
A program may use at most 64 MiB of HBM per device.

```python
import math
import jax
import jax.numpy as jnp
from jax import lax

INPUT_FEATURES = 4096
KEY_HEADS = 4
QPK = 8
HEAD_DIM = 128
ADAPTER_RANK = 64
STEPS = 1
SLOTS = 96
CTX = 16
ADAPTER_TOTAL = 8
ROWS = 768
HOME_CAP = 24
N_REPLICA = 8


def shared_order(key):
    return jax.random.permutation(jax.random.fold_in(key, 77), ADAPTER_TOTAL).astype(jnp.int32)


def cache_base(key):
    values = jax.random.normal(jax.random.fold_in(key, 11), (ROWS, KEY_HEADS, CTX, HEAD_DIM), jnp.float32)
    return jnp.clip(values, -6.0, 6.0)


def draw_adapter_replica(key, part):
    shuffled = shared_order(key)
    return shuffled


def draw_request_adapter(key, part):
    shuffled = shared_order(key)
    key = jax.random.fold_in(key, 2)
    entries_count = N_REPLICA * HOME_CAP
    candidate_list = jnp.tile(jnp.arange(N_REPLICA, dtype=jnp.int32), HOME_CAP)
    busiest_rank = jax.random.permutation(jax.random.fold_in(key, 5), N_REPLICA).astype(jnp.int32)
    extra_credit = jnp.where(busiest_rank == 0, 2, jnp.where(busiest_rank < max(1, N_REPLICA // 8), 1, 0)).astype(jnp.int32)
    jitter_values = jax.random.randint(jax.random.fold_in(key, 6), (N_REPLICA, entries_count), 0, entries_count)
    logit_scores = extra_credit[candidate_list][None, :] * (entries_count * entries_count + entries_count) + jitter_values * entries_count + jnp.arange(entries_count, dtype=jnp.int32)[None, :]
    picked = jnp.argsort(-logit_scores, axis=1)[:, :SLOTS]
    chosen_homes = candidate_list[picked]
    rest_count = SLOTS - HOME_CAP
    mixing = jax.random.randint(jax.random.fold_in(key, 7), (N_REPLICA, rest_count), 0, 1 << 20)
    mixing = mixing * rest_count + jnp.arange(rest_count, dtype=jnp.int32)[None, :]
    rest_order = jnp.argsort(mixing, axis=1)
    rest_homes = jnp.take_along_axis(chosen_homes[:, HOME_CAP:], rest_order, axis=1)
    chosen_homes = jnp.concatenate([chosen_homes[:, :HOME_CAP], rest_homes], axis=1)
    inverse = jnp.argsort(shuffled).astype(jnp.int32)
    return inverse[chosen_homes].reshape(-1).astype(jnp.int32)


def draw_replica_slot_count(key, part):
    key = jax.random.fold_in(key, 8)
    loads = jax.random.randint(jax.random.fold_in(key, 1), (N_REPLICA,), 7 * SLOTS // 8, SLOTS + 1)
    fullest = jax.random.randint(jax.random.fold_in(key, 2), (), 0, N_REPLICA)
    return loads.at[fullest].set(SLOTS).astype(jnp.int32)


def draw_cache_length(key, part):
    key = jax.random.fold_in(key, 9)
    lengths = jax.random.randint(jax.random.fold_in(key, 1), (ROWS,), 2, CTX + 1)
    longest = jax.random.randint(jax.random.fold_in(key, 2), (), 0, ROWS)
    return lengths.at[longest].set(CTX).astype(jnp.int32)


def draw_stored_key_cache(key, part):
    cached = cache_base(key)
    return cached.astype(jnp.bfloat16)


def draw_queries(key, part):
    key = jax.random.fold_in(key, 4)
    values = jax.random.normal(jax.random.fold_in(key, 1), (ROWS, STEPS, KEY_HEADS, QPK, HEAD_DIM), jnp.float32)
    values = jnp.clip(values, -6.0, 6.0)
    return values.reshape(ROWS, STEPS, KEY_HEADS, QPK * HEAD_DIM).astype(jnp.bfloat16)


def levels(own_key, shape, cuts, least, top_value):
    gain = 1.0
    for position, blocks in cuts:
        heights = jax.random.uniform(jax.random.fold_in(jax.random.fold_in(own_key, 6), position), (blocks,), jnp.float32, least / len(cuts), top_value / len(cuts))
        gain = gain * jnp.repeat(jnp.exp(heights), shape[position] // blocks).reshape((-1,) + (1,) * (len(shape) - 1 - position))
    return gain


def gaussian(own_key, shape, width, bound, shards=(), held_as=jnp.bfloat16):
    values = width * jax.random.normal(own_key, shape, jnp.float32)
    if shards:
        values = values * levels(own_key, shape, shards, -0.22, 0.18)
    return jnp.clip(values, -bound, bound).astype(held_as)


def setup_inputs(seed: int = 0, part: int = 0) -> dict:
    streams_of = jax.random.split(jax.random.key(seed), 13)
    part_splits = jax.random.split(jax.random.fold_in(streams_of[12], part), 13)
    return {
        "hidden": gaussian(part_splits[0], (ROWS, STEPS, INPUT_FEATURES), 1.0, 6.0, ((0, 8), (2, 2))),
        "queries": draw_queries(jax.random.fold_in(jax.random.fold_in(streams_of[12], part), 71), part),
        "incoming_keys": gaussian(part_splits[2], (ROWS, STEPS, KEY_HEADS, HEAD_DIM), 1.0, 6.0, ((0, 8), (2, 2))),
        "stored_key_cache": draw_stored_key_cache(jax.random.fold_in(jax.random.fold_in(streams_of[12], part), 71), part),
        "stored_value_cache": gaussian(part_splits[4], (ROWS, KEY_HEADS, CTX, HEAD_DIM), 1.0, 6.0, ((0, 8), (1, 2))),
        "base_value_weight": gaussian(streams_of[5], (INPUT_FEATURES, KEY_HEADS * HEAD_DIM), INPUT_FEATURES ** -0.5, 0.09375, ((0, 2),)),
        "adapter_down_rows": gaussian(streams_of[6], (ADAPTER_TOTAL, ADAPTER_RANK, INPUT_FEATURES), INPUT_FEATURES ** -0.5, 0.09375, ((0, 8), (2, 2))),
        "adapter_up_rows": gaussian(streams_of[7], (ADAPTER_TOTAL, ADAPTER_RANK, KEY_HEADS * HEAD_DIM), ADAPTER_RANK ** -0.5, 0.75, ((0, 8), (2, 2))),
        "request_adapter": draw_request_adapter(jax.random.fold_in(streams_of[12], 71), part),
        "adapter_replica": draw_adapter_replica(jax.random.fold_in(streams_of[12], 71), part),
        "replica_slot_count": draw_replica_slot_count(jax.random.fold_in(streams_of[12], 71), part),
        "cache_length": draw_cache_length(jax.random.fold_in(streams_of[12], 71), part),
    }


def attend(query_rows, fresh_keys, cached_keys, cached_values, fresh_values, lengths):
    row_count, step_count, head_count, query_width = query_rows.shape
    head_size = cached_keys.shape[3]
    grouped = query_rows.reshape(row_count, step_count, head_count, query_width // head_size, head_size).astype(jnp.float32)
    score_scale = 1.0 / math.sqrt(head_size)
    cache_scores = jnp.einsum('rsghd,rgpd->rsghp', grouped, cached_keys.astype(jnp.float32)) * score_scale
    fresh_scores = jnp.einsum('rsghd,rjgd->rsghj', grouped, fresh_keys.astype(jnp.float32)) * score_scale
    places = jnp.arange(cached_keys.shape[2], dtype=jnp.int32)
    cache_valid = places[None, :] < lengths[:, None]
    step_index = jnp.arange(step_count, dtype=jnp.int32)
    step_valid = step_index[None, :] <= step_index[:, None]
    cache_scores = jnp.where(cache_valid[:, None, None, None, :], cache_scores, -1e+30)
    fresh_scores = jnp.where(step_valid[None, :, None, None, :], fresh_scores, -1e+30)
    row_max = jnp.maximum(lax.optimization_barrier(jnp.max(cache_scores, axis=-1)), lax.optimization_barrier(jnp.max(fresh_scores, axis=-1)))[..., None]
    cache_exp = jnp.exp(cache_scores - row_max)
    fresh_exp = jnp.exp(fresh_scores - row_max)
    totals = lax.optimization_barrier(jnp.sum(cache_exp, axis=-1, keepdims=True)) + lax.optimization_barrier(jnp.sum(fresh_exp, axis=-1, keepdims=True))
    cache_weights = (cache_exp / totals).astype(jnp.bfloat16)
    fresh_weights = (fresh_exp / totals).astype(jnp.bfloat16)
    mixed = jnp.einsum('rsghp,rgpd->rsghd', cache_weights.astype(jnp.float32), cached_values.astype(jnp.float32))
    mixed = mixed + jnp.einsum('rsghj,rjgd->rsghd', fresh_weights.astype(jnp.float32), fresh_values.astype(jnp.float32))
    return mixed.reshape(row_count, step_count, head_count, query_width).astype(jnp.bfloat16)

def reference(hidden, queries, incoming_keys, stored_key_cache, stored_value_cache, base_value_weight, adapter_down_rows, adapter_up_rows, request_adapter, adapter_replica, replica_slot_count, cache_length):
    row_count = hidden.shape[0]
    block_count = row_count // SLOTS
    matches = request_adapter[:, None] == jnp.arange(ADAPTER_TOTAL, dtype=jnp.int32)[None, :]
    homes = lax.optimization_barrier(jnp.sum(jnp.where(matches, adapter_replica[None, :], 0), axis=1)).astype(jnp.int32)

    def split_rows(array):
        return array.reshape((block_count, SLOTS) + array.shape[1:])

    def one_block(packed):
        rows_in, query_rows, fresh_keys, cached_keys, cached_values, block_replicas, load_here, lengths = packed
        base_part = jnp.dot(rows_in.reshape(SLOTS * STEPS, INPUT_FEATURES), base_value_weight, preferred_element_type=jnp.float32)
        base_part = base_part.reshape(SLOTS, STEPS, KEY_HEADS * HEAD_DIM)
        down_matrix = jnp.take(adapter_down_rows, block_replicas, axis=0).astype(jnp.float32)
        projected = jnp.einsum('ksd,kqd->ksq', rows_in.astype(jnp.float32), down_matrix)
        shrunk = lax.optimization_barrier(projected.astype(jnp.bfloat16)).astype(jnp.float32)
        up_matrix = jnp.take(adapter_up_rows, block_replicas, axis=0).astype(jnp.float32)
        delta = jnp.einsum('ksq,kqe->kse', shrunk, up_matrix)
        live_mask = jnp.arange(SLOTS, dtype=jnp.int32) < load_here
        fresh_values = jnp.where(live_mask[:, None, None], base_part + delta, 0.0).astype(jnp.bfloat16)
        fresh_values = fresh_values.reshape(SLOTS, STEPS, KEY_HEADS, HEAD_DIM)
        mixed = attend(query_rows, fresh_keys, cached_keys, cached_values, fresh_values, lengths)
        mixed = jnp.where(live_mask[:, None, None, None], mixed, jnp.zeros_like(mixed))
        return (mixed, fresh_values)
    packed = (split_rows(hidden), split_rows(queries), split_rows(incoming_keys), split_rows(stored_key_cache), split_rows(stored_value_cache), split_rows(homes), replica_slot_count, split_rows(cache_length))
    mixed, fresh_values = lax.map(one_block, packed)
    attention = mixed.reshape(row_count, STEPS, KEY_HEADS, QPK * HEAD_DIM)
    new_values = fresh_values.reshape(row_count, STEPS, KEY_HEADS, HEAD_DIM)
    return (attention, new_values)
```

```python
import functools
import math

import jax
import jax.numpy as jnp
from jax import lax
from jax.experimental import pallas as pl
from jax.experimental.pallas import tpu as pltpu
from jax.sharding import PartitionSpec as P

NEGATIVE = -1e30
GATHER_BYTES = 1 << 22


def swap(array, axis, bit):
    size = lax.axis_size(axis)
    return lax.ppermute(array, axis, [(i, i ^ bit) for i in range(size)])


def cached_kernel(dims, lengths_ref, scalars_ref, hidden_ref, weight_ref, query_ref, key_ref, fresh_ref, value_ref,
                  kept_ref, sent_ref, mixed_ref, share_ref, total_ref):
    heads, query_heads, context, group, steps, scale = dims
    step = pl.program_id(0)
    product = jnp.dot(hidden_ref[...], weight_ref[...], preferred_element_type=jnp.float32)

    @pl.when(step == 0)
    def _():
        total_ref[...] = product

    @pl.when(step > 0)
    def _():
        total_ref[...] += product

    @pl.when(step == steps - 1)
    def _():
        columns = kept_ref.shape[1]
        low, high = total_ref[:, :columns], total_ref[:, columns:]
        first = scalars_ref[1] == 0
        kept_ref[...] = jnp.where(first, low, high)
        sent_ref[...] = jnp.where(first, high, low)

    slots = group // heads
    rows, places = group * query_heads, group * context
    blocks = query_ref.shape[0] // rows
    contract = (((1,), (1,)), ((), ()))

    def pair_of(shape):
        row = lax.broadcasted_iota(jnp.int32, shape, 0)
        return row // (heads * query_heads) * heads + row % heads

    own = pair_of((rows, places)) == lax.broadcasted_iota(jnp.int32, (rows, places), 1) // context
    lane = lax.broadcasted_iota(jnp.int32, (1, places), 1)
    query = query_ref[...]
    fresh = lax.dot_general(query, fresh_ref[...], contract, preferred_element_type=jnp.float32) * scale
    own_fresh = pair_of(fresh.shape) == lax.broadcasted_iota(jnp.int32, fresh.shape, 1)
    fresh = jnp.sum(jnp.where(own_fresh, fresh, 0.0), axis=1, keepdims=True)
    scores = []
    for block in range(blocks):
        base = (step * blocks + block) * slots
        keys = key_ref[pl.ds(block * places, places), :]
        score = lax.dot_general(
            query[block * rows : (block + 1) * rows], keys, contract, preferred_element_type=jnp.float32
        )
        limit = jnp.full((1, places), lengths_ref[base], jnp.int32)
        for s in range(1, slots):
            limit = jnp.where(lane // (heads * context) == s, lengths_ref[base + s], limit)
        scores.append(jnp.where(own & (lane % context < limit), score * scale, NEGATIVE))
    scores = jnp.concatenate(scores, axis=0)
    top = jnp.maximum(jnp.max(scores, axis=1, keepdims=True), fresh)
    parts = jnp.exp(scores - top)
    fresh_part = jnp.exp(fresh - top)
    inverse = 1.0 / (jnp.sum(parts, axis=1, keepdims=True) + fresh_part)
    row_slot = lax.broadcasted_iota(jnp.int32, inverse.shape, 0) // (heads * query_heads)
    inverse = jnp.where(step * blocks * slots + row_slot < scalars_ref[0], inverse, 0.0)
    weights = (parts * inverse).astype(jnp.bfloat16)
    mixed = [
        jnp.dot(
            weights[block * rows : (block + 1) * rows],
            value_ref[pl.ds(block * places, places), :],
            preferred_element_type=jnp.float32,
        )
        for block in range(blocks)
    ]
    mixed_ref[...] = jnp.concatenate(mixed, axis=0)
    share_ref[...] = jnp.where(own_fresh, fresh_part * inverse, 0.0).astype(share_ref.dtype)


def base_and_cached(rows, weight, query_rows, fresh_keys, cached_keys, cached_values, lengths, scalars):
    slots, features = rows.shape
    heads, context, size = cached_keys.shape[1:]
    query_heads = query_rows.shape[0] // (slots * heads)
    group, steps = 8, 4
    columns = weight.shape[1] // 2
    pairs = slots * heads
    dims = (heads, query_heads, context, group, steps, 1.0 / math.sqrt(size))
    return pl.pallas_call(
        functools.partial(cached_kernel, dims),
        grid_spec=pltpu.PrefetchScalarGridSpec(
            num_scalar_prefetch=2,
            grid=(steps,),
            in_specs=[
                pl.BlockSpec((slots, features // steps), lambda i, *_: (0, i)),
                pl.BlockSpec((features // steps, 2 * columns), lambda i, *_: (i, 0)),
                pl.BlockSpec((pairs * query_heads // steps, size), lambda i, *_: (i, 0)),
                pl.BlockSpec((pairs * context // steps, size), lambda i, *_: (i, 0)),
                pl.BlockSpec((pairs // steps, size), lambda i, *_: (i, 0)),
                pl.BlockSpec((pairs * context // steps, size), lambda i, *_: (i, 0)),
            ],
            out_specs=[
                pl.BlockSpec((slots, columns), lambda i, *_: (0, 0)),
                pl.BlockSpec((slots, columns), lambda i, *_: (0, 0)),
                pl.BlockSpec((pairs * query_heads // steps, size), lambda i, *_: (i, 0)),
                pl.BlockSpec((pairs * query_heads // steps, pairs // steps), lambda i, *_: (i, 0)),
            ],
            scratch_shapes=[pltpu.VMEM((slots, 2 * columns), jnp.float32)],
        ),
        out_shape=[
            jax.ShapeDtypeStruct((slots, columns), jnp.float32),
            jax.ShapeDtypeStruct((slots, columns), jnp.float32),
            jax.ShapeDtypeStruct(query_rows.shape, jnp.float32),
            jax.ShapeDtypeStruct((query_rows.shape[0], pairs // steps), jnp.bfloat16),
        ],
        compiler_params=pltpu.CompilerParams(vmem_limit_bytes=56 << 20),
        cost_estimate=pl.CostEstimate(flops=1 << 28, bytes_accessed=12 << 20, transcendentals=1 << 18),
    )(
        lengths,
        scalars,
        rows,
        weight,
        query_rows,
        cached_keys.reshape(pairs * context, size),
        fresh_keys.reshape(pairs, size),
        cached_values.reshape(pairs * context, size),
    )


def final_kernel(count_ref, own_ref, returned_ref, mixed_ref, share_ref, attention_ref, values_ref, spread_ref):
    slots = own_ref.shape[0]
    pairs, size = values_ref.shape
    heads = pairs // slots
    live = lax.broadcasted_iota(jnp.int32, (slots, 1), 0) < count_ref[0]
    fresh = jnp.where(live, own_ref[...] + returned_ref[...].astype(jnp.float32), 0.0)
    for head in range(heads):
        spread_ref[pl.ds(head, slots, stride=heads), :] = fresh[:, head * size : (head + 1) * size]
    values = spread_ref[...].astype(jnp.bfloat16)
    values_ref[...] = values
    group = share_ref.shape[1]
    rows = group * attention_ref.shape[0] // pairs
    for block in range(pairs // group):
        part = pl.ds(block * rows, rows)
        fresh_part = jnp.dot(
            share_ref[part, :], values[block * group : (block + 1) * group], preferred_element_type=jnp.float32
        )
        attention_ref[part, :] = (mixed_ref[part, :] + fresh_part).astype(attention_ref.dtype)


def finish(own, returned, mixed, share, live_count):
    slots, columns = own.shape
    size = mixed.shape[1]
    pairs = slots * columns // size
    vmem = pl.BlockSpec(memory_space=pltpu.VMEM)
    return pl.pallas_call(
        final_kernel,
        in_specs=[pl.BlockSpec(memory_space=pltpu.SMEM), vmem, vmem, vmem, vmem],
        out_specs=[vmem, vmem],
        out_shape=[
            jax.ShapeDtypeStruct(mixed.shape, jnp.bfloat16),
            jax.ShapeDtypeStruct((pairs, size), jnp.bfloat16),
        ],
        scratch_shapes=[pltpu.VMEM((pairs, size), jnp.float32)],
        compiler_params=pltpu.CompilerParams(vmem_limit_bytes=8 << 20),
    )(live_count, own, returned, mixed, share)


def moved_delta(rows, down, up, homes, live_mask):
    slots, features = rows.shape
    replicas = lax.axis_size("replica")
    capacity = max(2, 2 * slots // replicas)
    index = jnp.arange(slots, dtype=jnp.int32)
    earlier = (homes[:, None] == homes[None, :]) & live_mask[None, :] & (index[None, :] < index[:, None])
    position = jnp.sum(earlier.astype(jnp.int32), axis=1)
    target = jnp.where(live_mask, homes * capacity + position, replicas * capacity)
    outgoing = jnp.zeros((replicas * capacity, features), jnp.bfloat16).at[target].set(rows, mode="drop")
    arrived = lax.all_to_all(outgoing, "replica", split_axis=0, concat_axis=0, tiled=True)
    part = jnp.einsum("nd,qd->nq", arrived, down, preferred_element_type=jnp.float32)
    shrunk = lax.psum(part, "tensor").astype(jnp.bfloat16)
    delta = jnp.dot(shrunk, up, preferred_element_type=jnp.float32)
    returned = lax.all_to_all(delta, "replica", split_axis=0, concat_axis=0, tiled=True)
    return jnp.take(returned, target, axis=0, mode="clip")


def rank_kernel(offsets, half, ids_ref, rows_ref, other_ref, homes_ref, other_homes_ref, down_ref, *rest):
    mine, theirs = rest[: len(offsets) - 1], rest[len(offsets) - 1 : -2]
    ranks_ref, panel_ref = rest[-2:]
    rank = 2 * half
    panel_ref[pl.ds(0, rank), :] = down_ref[...]
    for k in range(1, len(offsets)):
        at = pl.multiple_of(k * rank + ids_ref[0], half)
        panel_ref[pl.ds(at, half), :] = mine[k - 1][...]
        at = pl.multiple_of(k * rank + half - ids_ref[0], half)
        panel_ref[pl.ds(at, half), :] = theirs[k - 1][...]
    contract = (((1,), (1,)), ((), ()))
    for i, (rows, homes) in enumerate(((rows_ref, homes_ref), (other_ref, other_homes_ref))):
        product = lax.dot_general(panel_ref[...], rows[...], contract, preferred_element_type=jnp.float32)
        total = jnp.zeros((rank, product.shape[1]), jnp.float32)
        for k in range(len(offsets)):
            here = homes[...] == ids_ref[1 + k]
            total += jnp.where(here, product[k * rank : (k + 1) * rank], 0.0)
        ranks_ref[pl.ds(i * rank, rank), :] = total


def delta_kernel(count, ids_ref, homes_ref, other_homes_ref, ranks_ref, got_ref, kept_ref, base_ref, *rest):
    ups = rest[:count]
    own_ref, sent_ref, panel_ref = rest[count:]
    rank = ranks_ref.shape[0] // 2
    for k in range(count):
        panel_ref[pl.ds(k * rank, rank), :] = ups[k][...]
    contract = (((0,), (0,)), ((), ()))
    summed = ranks_ref[...] + got_ref[...]
    for i, homes in enumerate((homes_ref, other_homes_ref)):
        shrunk = summed[i * rank : (i + 1) * rank]
        spread = jnp.concatenate([jnp.where(homes[...] == ids_ref[1 + k], shrunk, 0.0) for k in range(count)], axis=0)
        delta = lax.dot_general(spread.astype(jnp.bfloat16), panel_ref[...], contract, preferred_element_type=jnp.float32)
        if i == 0:
            own_ref[...] = delta + (kept_ref[...] + base_ref[...])
        else:
            sent_ref[...] = delta.astype(sent_ref.dtype)


def gathered_values(rows, down, up, homes, base_kept, base_sent):
    slots, features = rows.shape
    rank, columns = up.shape
    replicas = lax.axis_size("replica")
    half = rank // 2
    outer, inner = lax.axis_index("replica") // 2, lax.axis_index("replica") % 2
    start = lax.axis_index("group") * half
    held = [(0, lax.dynamic_slice_in_dim(down, start, half, 0), up)]
    bit = replicas // 4
    while bit:
        came = [(offset ^ bit, swap(part, "replica", 2 * bit), swap(raised, "replica", 2 * bit)) for offset, part, raised in held]
        if len(held) == 1:
            offset, *parts = came[0]
            parts, base_sent = lax.optimization_barrier((parts, base_sent))
            came = [(offset, *parts)]
        held = held + came
        bit //= 2
    base_got = swap(base_sent, "tensor", 1)
    offsets = [offset for offset, _, _ in held]
    mine = [part for _, part, _ in held[1:]]
    theirs = [swap(part, "group", 1) for part in mine]
    ups = [raised for _, _, raised in held]
    other_rows = swap(rows, "replica", 1)
    homes = homes[None, :]
    other_homes = swap(homes, "replica", 1)
    ids = jnp.stack([start] + [(outer ^ offset) * 2 + inner for offset in offsets]).astype(jnp.int32)
    vmem = pl.BlockSpec(memory_space=pltpu.VMEM)
    smem = pl.BlockSpec(memory_space=pltpu.SMEM)
    inputs = [rows, other_rows, homes, other_homes, down] + mine + theirs
    ranks = pl.pallas_call(
        functools.partial(rank_kernel, offsets, half),
        in_specs=[smem] + [vmem] * len(inputs),
        out_specs=vmem,
        out_shape=jax.ShapeDtypeStruct((2 * rank, slots), jnp.float32),
        scratch_shapes=[pltpu.VMEM((len(offsets) * rank, features), jnp.bfloat16)],
        compiler_params=pltpu.CompilerParams(vmem_limit_bytes=16 << 20),
    )(ids, *inputs)
    inputs = [homes, other_homes, ranks, swap(ranks, "tensor", 1), base_kept, base_got] + ups
    own, sent = pl.pallas_call(
        functools.partial(delta_kernel, len(ups)),
        in_specs=[smem] + [vmem] * len(inputs),
        out_specs=[vmem, vmem],
        out_shape=[
            jax.ShapeDtypeStruct((slots, columns), jnp.float32),
            jax.ShapeDtypeStruct((slots, columns), jnp.bfloat16),
        ],
        scratch_shapes=[pltpu.VMEM((len(ups) * rank, columns), jnp.bfloat16)],
        compiler_params=pltpu.CompilerParams(vmem_limit_bytes=16 << 20),
    )(ids, *inputs)
    return own, swap(sent, "replica", 1)


def local(
    hidden,
    queries,
    incoming_keys,
    stored_key_cache,
    stored_value_cache,
    base_value_weight,
    adapter_down_rows,
    adapter_up_rows,
    request_adapter,
    adapter_replica,
    replica_slot_count,
    cache_length,
):
    slots, _, features = hidden.shape
    heads, _, size = stored_key_cache.shape[1:]
    query_heads = queries.shape[3] // size
    replicas = lax.axis_size("replica")
    matches = request_adapter[:, None] == jnp.arange(adapter_replica.shape[0], dtype=jnp.int32)[None, :]
    homes = jnp.sum(jnp.where(matches, adapter_replica[None, :], 0), axis=1)
    rows = hidden.reshape(slots, features)
    down, up = adapter_down_rows[0], adapter_up_rows[0]
    query_rows = queries.reshape(slots, heads, query_heads, size).transpose(0, 2, 1, 3).reshape(-1, size)
    scalars = jnp.stack([replica_slot_count[0], lax.axis_index("tensor")]).astype(jnp.int32)
    base_kept, base_sent, mixed, share = base_and_cached(
        rows, base_value_weight, query_rows, incoming_keys, stored_key_cache, stored_value_cache, cache_length, scalars
    )
    power = replicas >= 4 and replicas & (replicas - 1) == 0
    if power and lax.axis_size("group") == 2 and replicas * down.size <= GATHER_BYTES:
        own, returned = gathered_values(rows, down, up, homes, base_kept, base_sent)
    else:
        live_mask = jnp.arange(slots, dtype=jnp.int32) < replica_slot_count[0]
        own, returned = base_kept + swap(base_sent, "tensor", 1), moved_delta(rows, down, up, homes, live_mask)
    attention, fresh_values = finish(own, returned, mixed, share, replica_slot_count)
    attention = attention.reshape(slots, query_heads, heads, size).transpose(0, 2, 1, 3)
    return (
        attention.reshape(slots, 1, heads, query_heads * size),
        fresh_values.reshape(slots, 1, heads, size),
    )


def solution(mesh):
    placed = (
        P(("group", "replica"), None, "tensor"),
        P(("group", "replica"), None, "tensor", None),
        P(("group", "replica"), None, "tensor", None),
        P(("group", "replica"), "tensor", None, None),
        P(("group", "replica"), "tensor", None, None),
        P("tensor", None),
        P("replica", None, "tensor"),
        P("replica", None, "tensor"),
        P("replica"),
        P(),
        P("replica"),
        P("replica"),
    )
    return jax.shard_map(
        local,
        mesh=mesh,
        in_specs=placed,
        out_specs=(
            P(("group", "replica"), None, "tensor", None),
            P(("group", "replica"), None, "tensor", None),
        ),
        check_vma=False,
    )
```

```python
import functools
import math

import jax
import jax.numpy as jnp
from jax import lax
from jax.experimental import pallas as pl
from jax.experimental.pallas import tpu as pltpu
from jax.sharding import PartitionSpec as P

NEGATIVE = -1e30
GATHER_BYTES = 1 << 22


def swap(array, axis, bit):
    size = lax.axis_size(axis)
    return lax.ppermute(array, axis, [(i, i ^ bit) for i in range(size)])


def cached_kernel(dims, lengths_ref, count_ref, *refs):
    heads, query_heads, context, group, parts, scale = dims
    sources, outputs, buffers, results = refs[:4], refs[4:6], refs[6:10], refs[10:12]
    in_sems, out_sems = refs[12:]

    def copy_of(source, target, sem, part):
        size = source.shape[0] // parts
        at = pl.ds(part * size, size)
        return pltpu.make_async_copy(source.at[at], target.at[at], sem)

    copies = [
        [copy_of(source, buffer, in_sems.at[part, i], part) for i, (source, buffer) in enumerate(zip(sources, buffers))]
        for part in range(parts)
    ]
    writes = [
        [copy_of(result, output, out_sems.at[part, i], part) for i, (result, output) in enumerate(zip(results, outputs))]
        for part in range(parts)
    ]
    for group_of_copies in copies:
        for copy in group_of_copies:
            copy.start()
    query_ref, key_ref, fresh_ref, value_ref = buffers
    mixed_ref, share_ref = results

    slots = group // heads
    rows, places = group * query_heads, group * context
    part_rows = query_ref.shape[0] // parts
    part_pairs = fresh_ref.shape[0] // parts
    blocks = part_rows // rows
    contract = (((1,), (1,)), ((), ()))

    def pair_of(shape):
        row = lax.broadcasted_iota(jnp.int32, shape, 0)
        return row // (heads * query_heads) * heads + row % heads

    own = pair_of((rows, places)) == lax.broadcasted_iota(jnp.int32, (rows, places), 1) // context
    own_fresh = pair_of((part_rows, part_pairs)) == lax.broadcasted_iota(jnp.int32, (part_rows, part_pairs), 1)
    row_slot = lax.broadcasted_iota(jnp.int32, (part_rows, 1), 0) // (heads * query_heads)
    lane = lax.broadcasted_iota(jnp.int32, (1, places), 1)
    for part in range(parts):
        for copy in copies[part]:
            copy.wait()
        query = query_ref[pl.ds(part * part_rows, part_rows), :]
        fresh_keys = fresh_ref[pl.ds(part * part_pairs, part_pairs), :]
        fresh = lax.dot_general(query, fresh_keys, contract, preferred_element_type=jnp.float32) * scale
        fresh = jnp.sum(jnp.where(own_fresh, fresh, 0.0), axis=1, keepdims=True)
        scores = []
        for block in range(blocks):
            base = (part * blocks + block) * slots
            keys = key_ref[pl.ds((part * blocks + block) * places, places), :]
            score = lax.dot_general(
                query[block * rows : (block + 1) * rows], keys, contract, preferred_element_type=jnp.float32
            )
            limit = jnp.full((1, places), lengths_ref[base], jnp.int32)
            for s in range(1, slots):
                limit = jnp.where(lane // (heads * context) == s, lengths_ref[base + s], limit)
            scores.append(jnp.where(own & (lane % context < limit), score * scale, NEGATIVE))
        scores = jnp.concatenate(scores, axis=0)
        top = jnp.maximum(jnp.max(scores, axis=1, keepdims=True), fresh)
        shares = jnp.exp(scores - top)
        fresh_share = jnp.exp(fresh - top)
        inverse = 1.0 / (jnp.sum(shares, axis=1, keepdims=True) + fresh_share)
        inverse = jnp.where(part * blocks * slots + row_slot < count_ref[0], inverse, 0.0)
        weights = (shares * inverse).astype(jnp.bfloat16)
        mixed = [
            jnp.dot(
                weights[block * rows : (block + 1) * rows],
                value_ref[pl.ds((part * blocks + block) * places, places), :],
                preferred_element_type=jnp.float32,
            )
            for block in range(blocks)
        ]
        mixed_ref[pl.ds(part * part_rows, part_rows), :] = jnp.concatenate(mixed, axis=0)
        share = jnp.where(own_fresh, fresh_share * inverse, 0.0)
        share_ref[pl.ds(part * part_rows, part_rows), :] = share.astype(share_ref.dtype)
        for write in writes[part]:
            write.start()
    for group_of_writes in writes:
        for write in group_of_writes:
            write.wait()


def cached_attention(query_rows, fresh_keys, cached_keys, cached_values, lengths, live_count):
    slots, heads, context, size = cached_keys.shape
    pairs = slots * heads
    query_heads = query_rows.shape[0] // pairs
    group, parts = 8, 4
    dims = (heads, query_heads, context, group, parts, 1.0 / math.sqrt(size))
    inputs = (
        query_rows,
        cached_keys.reshape(pairs * context, size),
        fresh_keys.reshape(pairs, size),
        cached_values.reshape(pairs * context, size),
    )
    outputs = [
        jax.ShapeDtypeStruct(query_rows.shape, jnp.float32),
        jax.ShapeDtypeStruct((query_rows.shape[0], pairs // parts), jnp.bfloat16),
    ]
    smem = pl.BlockSpec(memory_space=pltpu.SMEM)
    return pl.pallas_call(
        functools.partial(cached_kernel, dims),
        in_specs=[smem, smem] + [pl.BlockSpec(memory_space=pl.ANY)] * len(inputs),
        out_specs=[pl.BlockSpec(memory_space=pl.ANY)] * 2,
        out_shape=outputs,
        scratch_shapes=[pltpu.VMEM(x.shape, x.dtype) for x in (*inputs, *outputs)]
        + [pltpu.SemaphoreType.DMA((parts, len(inputs))), pltpu.SemaphoreType.DMA((parts, len(outputs)))],
        compiler_params=pltpu.CompilerParams(vmem_limit_bytes=56 << 20),
        cost_estimate=pl.CostEstimate(flops=1 << 28, bytes_accessed=6 << 20, transcendentals=1 << 18),
    )(lengths, live_count, *inputs)


def base_kernel(rows_ref, weight_ref, kept_ref, sent_ref):
    total = jnp.dot(rows_ref[...], weight_ref[...], preferred_element_type=jnp.float32)
    columns = kept_ref.shape[1]
    first = lax.axis_index("tensor") == 0
    kept_ref[...] = jnp.where(first, total[:, :columns], total[:, columns:])
    sent_ref[...] = jnp.where(first, total[:, columns:], total[:, :columns])


def base_sums(rows, weight):
    shape = jax.ShapeDtypeStruct((rows.shape[0], weight.shape[1] // 2), jnp.float32)
    vmem = pl.BlockSpec(memory_space=pltpu.VMEM)
    return pl.pallas_call(
        base_kernel,
        in_specs=[vmem, vmem],
        out_specs=[vmem, vmem],
        out_shape=[shape, shape],
        compiler_params=pltpu.CompilerParams(vmem_limit_bytes=8 << 20),
        cost_estimate=pl.CostEstimate(flops=1 << 28, bytes_accessed=3 << 20, transcendentals=0),
    )(rows, weight)


def final_kernel(count_ref, own_ref, returned_ref, mixed_ref, share_ref, attention_ref, values_ref, spread_ref):
    slots = own_ref.shape[0]
    pairs, size = values_ref.shape
    heads = pairs // slots
    live = lax.broadcasted_iota(jnp.int32, (slots, 1), 0) < count_ref[0]
    fresh = jnp.where(live, own_ref[...] + returned_ref[...].astype(jnp.float32), 0.0)
    for head in range(heads):
        spread_ref[pl.ds(head, slots, stride=heads), :] = fresh[:, head * size : (head + 1) * size]
    values = spread_ref[...].astype(jnp.bfloat16)
    values_ref[...] = values
    group = share_ref.shape[1]
    rows = group * attention_ref.shape[0] // pairs
    for block in range(pairs // group):
        part = pl.ds(block * rows, rows)
        fresh_part = jnp.dot(
            share_ref[part, :], values[block * group : (block + 1) * group], preferred_element_type=jnp.float32
        )
        attention_ref[part, :] = (mixed_ref[part, :] + fresh_part).astype(attention_ref.dtype)


def finish(own, returned, mixed, share, live_count):
    slots, columns = own.shape
    size = mixed.shape[1]
    pairs = slots * columns // size
    vmem = pl.BlockSpec(memory_space=pltpu.VMEM)
    return pl.pallas_call(
        final_kernel,
        in_specs=[pl.BlockSpec(memory_space=pltpu.SMEM), vmem, vmem, vmem, vmem],
        out_specs=[vmem, vmem],
        out_shape=[
            jax.ShapeDtypeStruct(mixed.shape, jnp.bfloat16),
            jax.ShapeDtypeStruct((pairs, size), jnp.bfloat16),
        ],
        scratch_shapes=[pltpu.VMEM((pairs, size), jnp.float32)],
        compiler_params=pltpu.CompilerParams(vmem_limit_bytes=8 << 20),
    )(live_count, own, returned, mixed, share)


def moved_delta(rows, down, up, homes, live_mask):
    slots, features = rows.shape
    replicas = lax.axis_size("replica")
    capacity = max(2, 2 * slots // replicas)
    index = jnp.arange(slots, dtype=jnp.int32)
    earlier = (homes[:, None] == homes[None, :]) & live_mask[None, :] & (index[None, :] < index[:, None])
    position = jnp.sum(earlier.astype(jnp.int32), axis=1)
    target = jnp.where(live_mask, homes * capacity + position, replicas * capacity)
    outgoing = jnp.zeros((replicas * capacity, features), jnp.bfloat16).at[target].set(rows, mode="drop")
    arrived = lax.all_to_all(outgoing, "replica", split_axis=0, concat_axis=0, tiled=True)
    part = jnp.einsum("nd,qd->nq", arrived, down, preferred_element_type=jnp.float32)
    shrunk = lax.psum(part, "tensor").astype(jnp.bfloat16)
    delta = jnp.dot(shrunk, up, preferred_element_type=jnp.float32)
    returned = lax.all_to_all(delta, "replica", split_axis=0, concat_axis=0, tiled=True)
    return jnp.take(returned, target, axis=0, mode="clip")


def home_masks(offsets, adapters, table_ref):
    homes = jnp.zeros(adapters.shape, jnp.int32)
    for adapter in range(table_ref.shape[0]):
        homes = jnp.where(adapters == adapter, table_ref[adapter], homes)
    place = lax.axis_index("replica")
    outer, inner = place // 2, place % 2
    return [homes == (outer ^ offset) * 2 + inner for offset in offsets]


def rank_kernel(offsets, half, table_ref, rows_ref, other_ref, adapters_ref, other_adapters_ref, down_ref, *rest):
    mine, theirs = rest[: len(offsets) - 1], rest[len(offsets) - 1 : -2]
    ranks_ref, panel_ref = rest[-2:]
    rank = 2 * half
    slots, features = rows_ref.shape
    start = lax.axis_index("group") * half
    panel_ref[pl.ds(0, rank), :] = down_ref[...]
    for k in range(1, len(offsets)):
        panel_ref[pl.ds(pl.multiple_of(k * rank + start, half), half), :] = mine[k - 1][:, :features]
        panel_ref[pl.ds(pl.multiple_of(k * rank + half - start, half), half), :] = theirs[k - 1][:, :features]
    contract = (((1,), (1,)), ((), ()))
    both = jnp.concatenate([rows_ref[...], other_ref[...]], axis=0)
    product = lax.dot_general(panel_ref[...], both, contract, preferred_element_type=jnp.float32)
    for i, adapters in enumerate((adapters_ref, other_adapters_ref)):
        total = jnp.zeros((rank, slots), jnp.float32)
        for k, here in enumerate(home_masks(offsets, adapters[...], table_ref)):
            total += jnp.where(here, product[k * rank : (k + 1) * rank, i * slots : (i + 1) * slots], 0.0)
        ranks_ref[pl.ds(i * rank, rank), :] = total


def delta_of(offsets, at, table_ref, adapters_ref, ranks_ref, got_ref, panel_ref):
    rank = ranks_ref.shape[0] // 2
    shrunk = ranks_ref[pl.ds(at * rank, rank), :] + got_ref[pl.ds(at * rank, rank), :]
    masks = home_masks(offsets, adapters_ref[...], table_ref)
    spread = jnp.concatenate([jnp.where(here, shrunk, 0.0) for here in masks], axis=0).astype(jnp.bfloat16)
    return lax.dot_general(spread, panel_ref[...], (((0,), (0,)), ((), ())), preferred_element_type=jnp.float32)


def sent_kernel(offsets, half, table_ref, adapters_ref, ranks_ref, got_ref, up_ref, *rest):
    mine, theirs = rest[: len(offsets) - 1], rest[len(offsets) - 1 : -2]
    sent_ref, panel_ref = rest[-2:]
    rank = 2 * half
    columns = sent_ref.shape[1]
    features = mine[0].shape[1] - columns
    start = lax.axis_index("group") * half
    panel_ref[pl.ds(0, rank), :] = up_ref[...]
    for k in range(1, len(offsets)):
        panel_ref[pl.ds(pl.multiple_of(k * rank + start, half), half), :] = mine[k - 1][:, features:]
        panel_ref[pl.ds(pl.multiple_of(k * rank + half - start, half), half), :] = theirs[k - 1][:, features:]
    sent_ref[...] = delta_of(offsets, 1, table_ref, adapters_ref, ranks_ref, got_ref, panel_ref).astype(sent_ref.dtype)


def own_kernel(offsets, table_ref, adapters_ref, ranks_ref, got_ref, panel_ref, kept_ref, base_ref, own_ref):
    delta = delta_of(offsets, 0, table_ref, adapters_ref, ranks_ref, got_ref, panel_ref)
    own_ref[...] = delta + (kept_ref[...] + base_ref[...])


def gathered_values(rows, weight, down, up, adapters, table, attention_inputs):
    slots, features = rows.shape
    rank, columns = up.shape
    replicas = lax.axis_size("replica")
    half = rank // 2
    adapters = adapters[None, :]
    vmem = pl.BlockSpec(memory_space=pltpu.VMEM)
    smem = pl.BlockSpec(memory_space=pltpu.SMEM)
    params = pltpu.CompilerParams(vmem_limit_bytes=16 << 20)
    start = lax.axis_index("group") * half
    packed = jnp.concatenate(
        [lax.dynamic_slice_in_dim(down, start, half, 0), lax.dynamic_slice_in_dim(up, start, half, 0)], axis=1
    )
    held = [(0, packed)]
    base_kept, base_sent = base_sums(rows, weight)
    other_adapters, sent_rows, base_sent = lax.optimization_barrier((swap(adapters, "replica", 1), rows, base_sent))
    other = swap(sent_rows, "replica", 1)
    near = swap(packed, "replica", 2)
    bit = replicas // 4
    while bit:
        came = [(offset ^ bit, swap(part, "replica", 2 * bit)) for offset, part in held if offset or bit > 1]
        if len(held) == 1:
            first, near, base_sent = lax.optimization_barrier((came[0][1], near, base_sent))
            came = [(came[0][0], first)]
        held = held + ([(1, near)] if bit == 1 else []) + came
        bit //= 2
    base_got = swap(base_sent, "tensor", 1)
    offsets = [offset for offset, _ in held]
    mine = [part for _, part in held[1:]]
    theirs = [swap(part, "group", 1) for part in mine]
    mine[-1], theirs[-2], query_rows = lax.optimization_barrier((mine[-1], theirs[-2], attention_inputs[0]))
    early = cached_attention(query_rows, *attention_inputs[1:])
    theirs[-1], early = lax.optimization_barrier((theirs[-1], early))
    inputs = [rows, other, adapters, other_adapters, down] + mine + theirs
    ranks = pl.pallas_call(
        functools.partial(rank_kernel, offsets, half),
        in_specs=[smem] + [vmem] * len(inputs),
        out_specs=vmem,
        out_shape=jax.ShapeDtypeStruct((2 * rank, slots), jnp.float32),
        scratch_shapes=[pltpu.VMEM((len(offsets) * rank, features), jnp.bfloat16)],
        compiler_params=params,
    )(table, *inputs)
    got = swap(ranks, "tensor", 1)
    inputs = [other_adapters, ranks, got, up] + mine + theirs
    sent, panel = pl.pallas_call(
        functools.partial(sent_kernel, offsets, half),
        in_specs=[smem] + [vmem] * len(inputs),
        out_specs=[vmem, vmem],
        out_shape=[
            jax.ShapeDtypeStruct((slots, columns), jnp.bfloat16),
            jax.ShapeDtypeStruct((len(offsets) * rank, columns), jnp.bfloat16),
        ],
        compiler_params=params,
    )(table, *inputs)
    returned = swap(sent, "replica", 1)
    inputs = [adapters, ranks, got, panel, base_kept, base_got]
    own = pl.pallas_call(
        functools.partial(own_kernel, offsets),
        in_specs=[smem] + [vmem] * len(inputs),
        out_specs=vmem,
        out_shape=jax.ShapeDtypeStruct((slots, columns), jnp.float32),
        compiler_params=params,
    )(table, *inputs)
    return own, returned, early


def local(
    hidden,
    queries,
    incoming_keys,
    stored_key_cache,
    stored_value_cache,
    base_value_weight,
    adapter_down_rows,
    adapter_up_rows,
    request_adapter,
    adapter_replica,
    replica_slot_count,
    cache_length,
):
    slots, _, features = hidden.shape
    heads, _, size = stored_key_cache.shape[1:]
    query_heads = queries.shape[3] // size
    replicas = lax.axis_size("replica")
    rows = hidden.reshape(slots, features)
    down, up = adapter_down_rows[0], adapter_up_rows[0]
    query_rows = queries.reshape(slots, heads, query_heads, size).transpose(0, 2, 1, 3).reshape(-1, size)
    attention_inputs = (
        query_rows, incoming_keys, stored_key_cache, stored_value_cache, cache_length, replica_slot_count
    )
    power = replicas >= 8 and replicas & (replicas - 1) == 0
    small = replicas * down.size <= GATHER_BYTES
    if power and small and lax.axis_size("group") == 2:
        own, returned, early = gathered_values(
            rows, base_value_weight, down, up, request_adapter, adapter_replica, attention_inputs
        )
    else:
        matches = request_adapter[:, None] == jnp.arange(adapter_replica.shape[0], dtype=jnp.int32)[None, :]
        homes = jnp.sum(jnp.where(matches, adapter_replica[None, :], 0), axis=1)
        live_mask = jnp.arange(slots, dtype=jnp.int32) < replica_slot_count[0]
        early = cached_attention(*attention_inputs)
        base_kept, base_sent = base_sums(rows, base_value_weight)
        own, returned = base_kept + swap(base_sent, "tensor", 1), moved_delta(rows, down, up, homes, live_mask)
    attention, fresh_values = finish(own, returned, *early, replica_slot_count)
    attention = attention.reshape(slots, query_heads, heads, size).transpose(0, 2, 1, 3)
    return (
        attention.reshape(slots, 1, heads, query_heads * size),
        fresh_values.reshape(slots, 1, heads, size),
    )


def solution(mesh):
    placed = (
        P(("group", "replica"), None, "tensor"),
        P(("group", "replica"), None, "tensor", None),
        P(("group", "replica"), None, "tensor", None),
        P(("group", "replica"), "tensor", None, None),
        P(("group", "replica"), "tensor", None, None),
        P("tensor", None),
        P("replica", None, "tensor"),
        P("replica", None, "tensor"),
        P("replica"),
        P(),
        P("replica"),
        P("replica"),
    )
    return jax.shard_map(
        local,
        mesh=mesh,
        in_specs=placed,
        out_specs=(
            P(("group", "replica"), None, "tensor", None),
            P(("group", "replica"), None, "tensor", None),
        ),
        check_vma=False,
    )
```

```python
import functools
import math

import jax
import jax.numpy as jnp
from jax import lax
from jax.experimental import pallas as pl
from jax.experimental.pallas import tpu as pltpu
from jax.sharding import PartitionSpec as P

NEGATIVE = -1e30
GATHER_BYTES = 1 << 22


def swap(array, axis, bit):
    size = lax.axis_size(axis)
    return lax.ppermute(array, axis, [(i, i ^ bit) for i in range(size)])


def cached_kernel(dims, lengths_ref, count_ref, *refs):
    heads, query_heads, context, group, parts, opening, scale = dims
    sources, outputs, buffers, results = refs[:4], refs[4:6], refs[6:10], refs[10:12]
    in_sems, out_sems = refs[12:]

    def copy_of(source, target, sem, part):
        size = min(source.shape[0], target.shape[0]) // parts
        begin = [(opening + part if ref.shape[0] > size * parts else part) * size for ref in (source, target)]
        return pltpu.make_async_copy(source.at[pl.ds(begin[0], size)], target.at[pl.ds(begin[1], size)], sem)

    copies = [
        [copy_of(source, buffer, in_sems.at[part, i], part) for i, (source, buffer) in enumerate(zip(sources, buffers))]
        for part in range(parts)
    ]
    writes = [
        [copy_of(result, output, out_sems.at[part, i], part) for i, (result, output) in enumerate(zip(results, outputs))]
        for part in range(parts)
    ]
    for group_of_copies in copies:
        for copy in group_of_copies:
            copy.start()
    query_ref, key_ref, fresh_ref, value_ref = buffers
    mixed_ref, share_ref = results

    slots = group // heads
    rows, places = group * query_heads, group * context
    part_rows = query_ref.shape[0] // parts
    part_pairs = fresh_ref.shape[0] // parts
    blocks = part_rows // rows
    contract = (((1,), (1,)), ((), ()))

    def pair_of(shape):
        row = lax.broadcasted_iota(jnp.int32, shape, 0)
        return row // (heads * query_heads) * heads + row % heads

    own = pair_of((rows, places)) == lax.broadcasted_iota(jnp.int32, (rows, places), 1) // context
    own_fresh = pair_of((part_rows, part_pairs)) == lax.broadcasted_iota(jnp.int32, (part_rows, part_pairs), 1)
    row_slot = lax.broadcasted_iota(jnp.int32, (part_rows, 1), 0) // (heads * query_heads)
    lane = lax.broadcasted_iota(jnp.int32, (1, places), 1)
    for part in range(parts):
        for copy in copies[part]:
            copy.wait()
        query = query_ref[pl.ds(part * part_rows, part_rows), :]
        fresh_keys = fresh_ref[pl.ds(part * part_pairs, part_pairs), :]
        fresh = lax.dot_general(query, fresh_keys, contract, preferred_element_type=jnp.float32) * scale
        fresh = jnp.sum(jnp.where(own_fresh, fresh, 0.0), axis=1, keepdims=True)
        scores = []
        for block in range(blocks):
            base = ((opening + part) * blocks + block) * slots
            keys = key_ref[pl.ds((part * blocks + block) * places, places), :]
            score = lax.dot_general(
                query[block * rows : (block + 1) * rows], keys, contract, preferred_element_type=jnp.float32
            )
            limit = jnp.full((1, places), lengths_ref[base], jnp.int32)
            for s in range(1, slots):
                limit = jnp.where(lane // (heads * context) == s, lengths_ref[base + s], limit)
            scores.append(jnp.where(own & (lane % context < limit), score * scale, NEGATIVE))
        scores = jnp.concatenate(scores, axis=0)
        top = jnp.maximum(jnp.max(scores, axis=1, keepdims=True), fresh)
        shares = jnp.exp(scores - top)
        fresh_share = jnp.exp(fresh - top)
        inverse = 1.0 / (jnp.sum(shares, axis=1, keepdims=True) + fresh_share)
        inverse = jnp.where((opening + part) * blocks * slots + row_slot < count_ref[0], inverse, 0.0)
        weights = (shares * inverse).astype(jnp.bfloat16)
        mixed = [
            jnp.dot(
                weights[block * rows : (block + 1) * rows],
                value_ref[pl.ds((part * blocks + block) * places, places), :],
                preferred_element_type=jnp.float32,
            )
            for block in range(blocks)
        ]
        mixed_ref[pl.ds(part * part_rows, part_rows), :] = jnp.concatenate(mixed, axis=0)
        share = jnp.where(own_fresh, fresh_share * inverse, 0.0)
        share_ref[pl.ds(part * part_rows, part_rows), :] = share.astype(share_ref.dtype)
        for write in writes[part]:
            write.start()
    for group_of_writes in writes:
        for write in group_of_writes:
            write.wait()


def cached_attention(opening, parts, query_rows, fresh_keys, cached_keys, cached_values, lengths, live_count):
    slots, heads, context, size = cached_keys.shape
    pairs = slots * heads
    query_heads = query_rows.shape[0] // pairs
    group, runs = 8, 2
    dims = (heads, query_heads, context, group, parts, opening, 1.0 / math.sqrt(size))
    inputs = (
        query_rows,
        cached_keys.reshape(pairs * context, size),
        fresh_keys.reshape(pairs, size),
        cached_values.reshape(pairs * context, size),
    )
    rows = query_rows.shape[0] // runs * parts
    outputs = [
        jax.ShapeDtypeStruct((rows, size), jnp.float32),
        jax.ShapeDtypeStruct((rows, pairs // runs), jnp.bfloat16),
    ]
    smem = pl.BlockSpec(memory_space=pltpu.SMEM)
    return pl.pallas_call(
        functools.partial(cached_kernel, dims),
        in_specs=[smem, smem] + [pl.BlockSpec(memory_space=pl.ANY)] * len(inputs),
        out_specs=[pl.BlockSpec(memory_space=pl.ANY)] * 2,
        out_shape=outputs,
        scratch_shapes=[pltpu.VMEM((x.shape[0] // runs * parts, x.shape[1]), x.dtype) for x in inputs]
        + [pltpu.VMEM(x.shape, x.dtype) for x in outputs]
        + [pltpu.SemaphoreType.DMA((parts, len(inputs))), pltpu.SemaphoreType.DMA((parts, len(outputs)))],
        compiler_params=pltpu.CompilerParams(vmem_limit_bytes=56 << 20),
        cost_estimate=pl.CostEstimate(flops=1 << 26, bytes_accessed=3 << 20, transcendentals=1 << 17),
    )(lengths, live_count, *inputs)


def base_kernel(rows_ref, weight_ref, kept_ref, sent_ref, copy_ref):
    copy_ref[...] = rows_ref[...]
    total = jnp.dot(rows_ref[...], weight_ref[...], preferred_element_type=jnp.float32)
    columns = kept_ref.shape[1]
    first = lax.axis_index("tensor") == 0
    kept_ref[...] = jnp.where(first, total[:, :columns], total[:, columns:])
    sent_ref[...] = jnp.where(first, total[:, columns:], total[:, :columns])


def base_sums(rows, weight):
    shape = jax.ShapeDtypeStruct((rows.shape[0], weight.shape[1] // 2), jnp.float32)
    vmem = pl.BlockSpec(memory_space=pltpu.VMEM)
    return pl.pallas_call(
        base_kernel,
        in_specs=[vmem, vmem],
        out_specs=[vmem, vmem, vmem],
        out_shape=[shape, shape, jax.ShapeDtypeStruct(rows.shape, rows.dtype)],
        compiler_params=pltpu.CompilerParams(vmem_limit_bytes=8 << 20),
        cost_estimate=pl.CostEstimate(flops=1 << 28, bytes_accessed=3 << 20, transcendentals=0),
    )(rows, weight)


def final_kernel(count_ref, own_ref, returned_ref, *rest):
    halves, (attention_ref, values_ref, spread_ref) = rest[:-3], rest[-3:]
    slots = own_ref.shape[0]
    pairs, size = values_ref.shape
    heads = pairs // slots
    live = lax.broadcasted_iota(jnp.int32, (slots, 1), 0) < count_ref[0]
    fresh = jnp.where(live, own_ref[...] + returned_ref[...].astype(jnp.float32), 0.0)
    for head in range(heads):
        spread_ref[pl.ds(head, slots, stride=heads), :] = fresh[:, head * size : (head + 1) * size]
    values = spread_ref[...].astype(jnp.bfloat16)
    values_ref[...] = values
    done = 0
    for mixed_ref, share_ref in zip(halves[::2], halves[1::2]):
        group = share_ref.shape[1]
        rows = group * attention_ref.shape[0] // pairs
        for begin in range(0, mixed_ref.shape[0], rows):
            fresh_part = jnp.dot(
                share_ref[pl.ds(begin, rows), :], values[done : done + group], preferred_element_type=jnp.float32
            )
            attended = mixed_ref[pl.ds(begin, rows), :] + fresh_part
            attention_ref[pl.ds(done // group * rows, rows), :] = attended.astype(attention_ref.dtype)
            done += group


def finish(own, returned, halves, live_count):
    slots, columns = own.shape
    size = halves[0].shape[1]
    pairs = slots * columns // size
    query_rows = sum(half.shape[0] for half in halves[::2])
    vmem = pl.BlockSpec(memory_space=pltpu.VMEM)
    return pl.pallas_call(
        final_kernel,
        in_specs=[pl.BlockSpec(memory_space=pltpu.SMEM), vmem, vmem] + [vmem] * len(halves),
        out_specs=[vmem, vmem],
        out_shape=[
            jax.ShapeDtypeStruct((query_rows, size), jnp.bfloat16),
            jax.ShapeDtypeStruct((pairs, size), jnp.bfloat16),
        ],
        scratch_shapes=[pltpu.VMEM((pairs, size), jnp.float32)],
        compiler_params=pltpu.CompilerParams(vmem_limit_bytes=8 << 20),
    )(live_count, own, returned, *halves)


def moved_delta(rows, down, up, homes, live_mask):
    slots, features = rows.shape
    replicas = lax.axis_size("replica")
    capacity = max(2, 2 * slots // replicas)
    index = jnp.arange(slots, dtype=jnp.int32)
    earlier = (homes[:, None] == homes[None, :]) & live_mask[None, :] & (index[None, :] < index[:, None])
    position = jnp.sum(earlier.astype(jnp.int32), axis=1)
    target = jnp.where(live_mask, homes * capacity + position, replicas * capacity)
    outgoing = jnp.zeros((replicas * capacity, features), jnp.bfloat16).at[target].set(rows, mode="drop")
    arrived = lax.all_to_all(outgoing, "replica", split_axis=0, concat_axis=0, tiled=True)
    part = jnp.einsum("nd,qd->nq", arrived, down, preferred_element_type=jnp.float32)
    shrunk = lax.psum(part, "tensor").astype(jnp.bfloat16)
    delta = jnp.dot(shrunk, up, preferred_element_type=jnp.float32)
    returned = lax.all_to_all(delta, "replica", split_axis=0, concat_axis=0, tiled=True)
    return jnp.take(returned, target, axis=0, mode="clip")


def home_masks(offsets, adapters, table_ref):
    homes = jnp.zeros(adapters.shape, jnp.int32)
    for adapter in range(table_ref.shape[0]):
        homes = jnp.where(adapters == adapter, table_ref[adapter], homes)
    place = lax.axis_index("replica")
    outer, inner = place // 2, place % 2
    return [homes == (outer ^ offset) * 2 + inner for offset in offsets]


def fill(panel_ref, columns, half, wholes, mine, theirs):
    rank = 2 * half
    start = lax.axis_index("group") * half
    for k, whole in enumerate(wholes):
        panel_ref[pl.ds(k * rank, rank), :] = whole[:, columns] if whole.shape[1] > panel_ref.shape[1] else whole[...]
    for k, (first, second) in enumerate(zip(mine, theirs), len(wholes)):
        panel_ref[pl.ds(pl.multiple_of(k * rank + start, half), half), :] = first[:, columns]
        panel_ref[pl.ds(pl.multiple_of(k * rank + half - start, half), half), :] = second[:, columns]


def rank_kernel(offsets, half, counts, table_ref, rows_ref, other_ref, adapters_ref, other_adapters_ref, *rest):
    wholes, mine, theirs = rest[: counts[0]], rest[counts[0] : sum(counts)], rest[sum(counts) : -2]
    ranks_ref, panel_ref = rest[-2:]
    rank = 2 * half
    slots, features = rows_ref.shape
    fill(panel_ref, slice(0, features), half, wholes, mine, theirs)
    contract = (((1,), (1,)), ((), ()))
    both = jnp.concatenate([rows_ref[...], other_ref[...]], axis=0)
    product = lax.dot_general(panel_ref[...], both, contract, preferred_element_type=jnp.float32)
    for i, adapters in enumerate((adapters_ref, other_adapters_ref)):
        total = jnp.zeros((rank, slots), jnp.float32)
        for k, here in enumerate(home_masks(offsets, adapters[...], table_ref)):
            total += jnp.where(here, product[k * rank : (k + 1) * rank, i * slots : (i + 1) * slots], 0.0)
        ranks_ref[pl.ds(i * rank, rank), :] = total


def delta_of(offsets, at, table_ref, adapters_ref, ranks_ref, got_ref, panel_ref):
    rank = ranks_ref.shape[0] // 2
    shrunk = ranks_ref[pl.ds(at * rank, rank), :] + got_ref[pl.ds(at * rank, rank), :]
    masks = home_masks(offsets, adapters_ref[...], table_ref)
    spread = jnp.concatenate([jnp.where(here, shrunk, 0.0) for here in masks], axis=0).astype(jnp.bfloat16)
    return lax.dot_general(spread, panel_ref[...], (((0,), (0,)), ((), ())), preferred_element_type=jnp.float32)


def sent_kernel(offsets, half, counts, table_ref, adapters_ref, ranks_ref, got_ref, *rest):
    wholes, mine, theirs = rest[: counts[0]], rest[counts[0] : sum(counts)], rest[sum(counts) : -2]
    sent_ref, panel_ref = rest[-2:]
    width = mine[0].shape[1]
    fill(panel_ref, slice(width - sent_ref.shape[1], width), half, wholes, mine, theirs)
    sent_ref[...] = delta_of(offsets, 1, table_ref, adapters_ref, ranks_ref, got_ref, panel_ref).astype(sent_ref.dtype)


def own_kernel(offsets, table_ref, adapters_ref, ranks_ref, got_ref, panel_ref, kept_ref, base_ref, own_ref):
    delta = delta_of(offsets, 0, table_ref, adapters_ref, ranks_ref, got_ref, panel_ref)
    own_ref[...] = delta + (kept_ref[...] + base_ref[...])


def gathered_values(rows, weight, down, up, adapters, table, attention_inputs):
    slots, features = rows.shape
    rank, columns = up.shape
    replicas = lax.axis_size("replica")
    half = rank // 2
    adapters = adapters[None, :]
    vmem = pl.BlockSpec(memory_space=pltpu.VMEM)
    smem = pl.BlockSpec(memory_space=pltpu.SMEM)
    params = pltpu.CompilerParams(vmem_limit_bytes=16 << 20)
    start = lax.axis_index("group") * half
    packed = jnp.concatenate(
        [lax.dynamic_slice_in_dim(down, start, half, 0), lax.dynamic_slice_in_dim(up, start, half, 0)], axis=1
    )
    base_kept, base_sent, rows_near = base_sums(rows, weight)
    other_adapters, sent_rows, base_sent = lax.optimization_barrier((swap(adapters, "replica", 1), rows, base_sent))
    other = swap(sent_rows, "replica", 1)
    near = swap(jnp.concatenate([down, up], axis=1), "replica", 2)
    query_rows, *attention_rest = attention_inputs
    held = [(0, packed)]
    bit = replicas // 4
    while bit:
        came = [(offset ^ bit, swap(part, "replica", 2 * bit)) for offset, part in held if offset or bit > 1]
        if len(held) == 1:
            first, base_sent, query_rows = lax.optimization_barrier((came[0][1], base_sent, query_rows))
            came = [(came[0][0], first)]
        held = held + came
        bit //= 2
    base_got = swap(base_sent, "tensor", 1)
    offsets = [0, 1] + [offset for offset, _ in held[1:]]
    mine = [part for _, part in held[1:]]
    theirs = [swap(part, "group", 1) for part in mine]
    mine[-1], theirs[-2], query_rows = lax.optimization_barrier((mine[-1], theirs[-2], query_rows))
    halves = cached_attention(0, 2, query_rows, *attention_rest)

    theirs[-1], halves = lax.optimization_barrier((theirs[-1], halves))
    inputs = [rows_near, other, adapters, other_adapters, down, near] + mine + theirs
    ranks = pl.pallas_call(
        functools.partial(rank_kernel, offsets, half, (2, len(mine))),
        in_specs=[smem] + [vmem] * len(inputs),
        out_specs=vmem,
        out_shape=jax.ShapeDtypeStruct((2 * rank, slots), jnp.float32),
        scratch_shapes=[pltpu.VMEM((len(offsets) * rank, features), jnp.bfloat16)],
        compiler_params=params,
    )(table, *inputs)
    got = swap(ranks, "tensor", 1)
    inputs = [other_adapters, ranks, got, up, near] + mine + theirs
    sent, panel = pl.pallas_call(
        functools.partial(sent_kernel, offsets, half, (2, len(mine))),
        in_specs=[smem] + [vmem] * len(inputs),
        out_specs=[vmem, vmem],
        out_shape=[
            jax.ShapeDtypeStruct((slots, columns), jnp.bfloat16),
            jax.ShapeDtypeStruct((len(offsets) * rank, columns), jnp.bfloat16),
        ],
        compiler_params=params,
    )(table, *inputs)
    returned = swap(sent, "replica", 1)
    inputs = [adapters, ranks, got, panel, base_kept, base_got]
    own = pl.pallas_call(
        functools.partial(own_kernel, offsets),
        in_specs=[smem] + [vmem] * len(inputs),
        out_specs=vmem,
        out_shape=jax.ShapeDtypeStruct((slots, columns), jnp.float32),
        compiler_params=params,
    )(table, *inputs)
    return own, returned, halves


def local(
    hidden,
    queries,
    incoming_keys,
    stored_key_cache,
    stored_value_cache,
    base_value_weight,
    adapter_down_rows,
    adapter_up_rows,
    request_adapter,
    adapter_replica,
    replica_slot_count,
    cache_length,
):
    slots, _, features = hidden.shape
    heads, _, size = stored_key_cache.shape[1:]
    query_heads = queries.shape[3] // size
    replicas = lax.axis_size("replica")
    rows = hidden.reshape(slots, features)
    down, up = adapter_down_rows[0], adapter_up_rows[0]
    query_rows = queries.reshape(slots, heads, query_heads, size).transpose(0, 2, 1, 3).reshape(-1, size)
    attention_inputs = (
        query_rows, incoming_keys, stored_key_cache, stored_value_cache, cache_length, replica_slot_count
    )
    power = replicas >= 8 and replicas & (replicas - 1) == 0
    small = replicas * down.size <= GATHER_BYTES
    if power and small and lax.axis_size("group") == 2:
        own, returned, halves = gathered_values(
            rows, base_value_weight, down, up, request_adapter, adapter_replica, attention_inputs
        )
    else:
        matches = request_adapter[:, None] == jnp.arange(adapter_replica.shape[0], dtype=jnp.int32)[None, :]
        homes = jnp.sum(jnp.where(matches, adapter_replica[None, :], 0), axis=1)
        live_mask = jnp.arange(slots, dtype=jnp.int32) < replica_slot_count[0]
        halves = cached_attention(0, 2, *attention_inputs)
        base_kept, base_sent, _ = base_sums(rows, base_value_weight)
        own, returned = base_kept + swap(base_sent, "tensor", 1), moved_delta(rows, down, up, homes, live_mask)
    attention, fresh_values = finish(own, returned, halves, replica_slot_count)
    attention = attention.reshape(slots, query_heads, heads, size).transpose(0, 2, 1, 3)
    return (
        attention.reshape(slots, 1, heads, query_heads * size),
        fresh_values.reshape(slots, 1, heads, size),
    )


def solution(mesh):
    placed = (
        P(("group", "replica"), None, "tensor"),
        P(("group", "replica"), None, "tensor", None),
        P(("group", "replica"), None, "tensor", None),
        P(("group", "replica"), "tensor", None, None),
        P(("group", "replica"), "tensor", None, None),
        P("tensor", None),
        P("replica", None, "tensor"),
        P("replica", None, "tensor"),
        P("replica"),
        P(),
        P("replica"),
        P("replica"),
    )
    return jax.shard_map(
        local,
        mesh=mesh,
        in_specs=placed,
        out_specs=(
            P(("group", "replica"), None, "tensor", None),
            P(("group", "replica"), None, "tensor", None),
        ),
        check_vma=False,
    )
```

```python
import functools
import math

import jax
import jax.numpy as jnp
from jax import lax
from jax.experimental import pallas as pl
from jax.experimental.pallas import tpu as pltpu
from jax.sharding import PartitionSpec as P

NEGATIVE = -1e30
GATHER_BYTES = 1 << 22


def swap(array, axis, bit):
    size = lax.axis_size(axis)
    return lax.ppermute(array, axis, [(i, i ^ bit) for i in range(size)])


def cached_kernel(dims, lengths_ref, count_ref, *refs):
    heads, query_heads, context, group, parts, opening, scale = dims
    query_ref, key_ref, fresh_ref, value_ref, mixed_ref, share_ref = refs
    slots = group // heads
    rows, places = group * query_heads, group * context
    part_rows = query_ref.shape[0] // parts
    part_pairs = fresh_ref.shape[0] // parts
    blocks = part_rows // rows
    contract = (((1,), (1,)), ((), ()))

    def pair_of(shape):
        row = lax.broadcasted_iota(jnp.int32, shape, 0)
        return row // (heads * query_heads) * heads + row % heads

    own = pair_of((rows, places)) == lax.broadcasted_iota(jnp.int32, (rows, places), 1) // context
    own_fresh = pair_of((part_rows, part_pairs)) == lax.broadcasted_iota(jnp.int32, (part_rows, part_pairs), 1)
    row_slot = lax.broadcasted_iota(jnp.int32, (part_rows, 1), 0) // (heads * query_heads)
    lane = lax.broadcasted_iota(jnp.int32, (1, places), 1)
    for part in range(parts):
        query = query_ref[pl.ds(part * part_rows, part_rows), :]
        fresh_keys = fresh_ref[pl.ds(part * part_pairs, part_pairs), :]
        fresh = lax.dot_general(query, fresh_keys, contract, preferred_element_type=jnp.float32) * scale
        fresh = jnp.sum(jnp.where(own_fresh, fresh, 0.0), axis=1, keepdims=True)
        scores = []
        for block in range(blocks):
            base = ((opening + part) * blocks + block) * slots
            keys = key_ref[pl.ds((part * blocks + block) * places, places), :]
            score = lax.dot_general(
                query[block * rows : (block + 1) * rows], keys, contract, preferred_element_type=jnp.float32
            )
            limit = jnp.full((1, places), lengths_ref[base], jnp.int32)
            for s in range(1, slots):
                limit = jnp.where(lane // (heads * context) == s, lengths_ref[base + s], limit)
            scores.append(jnp.where(own & (lane % context < limit), score * scale, NEGATIVE))
        scores = jnp.concatenate(scores, axis=0)
        top = jnp.maximum(jnp.max(scores, axis=1, keepdims=True), fresh)
        shares = jnp.exp(scores - top)
        fresh_share = jnp.exp(fresh - top)
        inverse = 1.0 / (jnp.sum(shares, axis=1, keepdims=True) + fresh_share)
        inverse = jnp.where((opening + part) * blocks * slots + row_slot < count_ref[0], inverse, 0.0)
        weights = (shares * inverse).astype(jnp.bfloat16)
        mixed = [
            jnp.dot(
                weights[block * rows : (block + 1) * rows],
                value_ref[pl.ds((part * blocks + block) * places, places), :],
                preferred_element_type=jnp.float32,
            )
            for block in range(blocks)
        ]
        mixed_ref[pl.ds(part * part_rows, part_rows), :] = jnp.concatenate(mixed, axis=0)
        share = jnp.where(own_fresh, fresh_share * inverse, 0.0)
        share_ref[pl.ds(part * part_rows, part_rows), :] = share.astype(share_ref.dtype)


def cached_attention(opening, parts, query_rows, fresh_keys, cached_keys, cached_values, lengths, live_count):
    slots, heads, context, size = cached_keys.shape
    pairs = slots * heads
    query_heads = query_rows.shape[0] // pairs
    group, runs = 8, 2
    dims = (heads, query_heads, context, group, parts, opening, 1.0 / math.sqrt(size))
    inputs = (
        query_rows,
        cached_keys.reshape(pairs * context, size),
        fresh_keys.reshape(pairs, size),
        cached_values.reshape(pairs * context, size),
    )
    rows = query_rows.shape[0] // runs * parts
    outputs = [
        jax.ShapeDtypeStruct((rows, size), jnp.float32),
        jax.ShapeDtypeStruct((rows, pairs // runs), jnp.bfloat16),
    ]
    smem = pl.BlockSpec(memory_space=pltpu.SMEM)
    vmem = pl.BlockSpec(memory_space=pltpu.VMEM)
    return pl.pallas_call(
        functools.partial(cached_kernel, dims),
        in_specs=[smem, smem] + [vmem] * len(inputs),
        out_specs=[vmem] * 2,
        out_shape=outputs,
        compiler_params=pltpu.CompilerParams(vmem_limit_bytes=16 << 20),
        cost_estimate=pl.CostEstimate(flops=1 << 26, bytes_accessed=3 << 20, transcendentals=1 << 17),
    )(lengths, live_count, *inputs)


def base_kernel(rows_ref, weight_ref, kept_ref, sent_ref, copy_ref):
    copy_ref[...] = rows_ref[...]
    total = jnp.dot(rows_ref[...], weight_ref[...], preferred_element_type=jnp.float32)
    columns = kept_ref.shape[1]
    first = lax.axis_index("tensor") == 0
    kept_ref[...] = jnp.where(first, total[:, :columns], total[:, columns:])
    sent_ref[...] = jnp.where(first, total[:, columns:], total[:, :columns])


def base_sums(rows, weight):
    shape = jax.ShapeDtypeStruct((rows.shape[0], weight.shape[1] // 2), jnp.float32)
    vmem = pl.BlockSpec(memory_space=pltpu.VMEM)
    return pl.pallas_call(
        base_kernel,
        in_specs=[vmem, vmem],
        out_specs=[vmem, vmem, vmem],
        out_shape=[shape, shape, jax.ShapeDtypeStruct(rows.shape, rows.dtype)],
        compiler_params=pltpu.CompilerParams(vmem_limit_bytes=8 << 20),
        cost_estimate=pl.CostEstimate(flops=1 << 28, bytes_accessed=3 << 20, transcendentals=0),
    )(rows, weight)


def final_kernel(count_ref, own_ref, returned_ref, *rest):
    halves, (attention_ref, values_ref, spread_ref) = rest[:-3], rest[-3:]
    slots = own_ref.shape[0]
    pairs, size = values_ref.shape
    heads = pairs // slots
    live = lax.broadcasted_iota(jnp.int32, (slots, 1), 0) < count_ref[0]
    fresh = jnp.where(live, own_ref[...] + returned_ref[...].astype(jnp.float32), 0.0)
    for head in range(heads):
        spread_ref[pl.ds(head, slots, stride=heads), :] = fresh[:, head * size : (head + 1) * size]
    values = spread_ref[...].astype(jnp.bfloat16)
    values_ref[...] = values
    done = 0
    for mixed_ref, share_ref in zip(halves[::2], halves[1::2]):
        group = share_ref.shape[1]
        rows = group * attention_ref.shape[0] // pairs
        for begin in range(0, mixed_ref.shape[0], rows):
            fresh_part = jnp.dot(
                share_ref[pl.ds(begin, rows), :], values[done : done + group], preferred_element_type=jnp.float32
            )
            attended = mixed_ref[pl.ds(begin, rows), :] + fresh_part
            attention_ref[pl.ds(done // group * rows, rows), :] = attended.astype(attention_ref.dtype)
            done += group


def finish(own, returned, halves, live_count):
    slots, columns = own.shape
    size = halves[0].shape[1]
    pairs = slots * columns // size
    query_rows = sum(half.shape[0] for half in halves[::2])
    vmem = pl.BlockSpec(memory_space=pltpu.VMEM)
    return pl.pallas_call(
        final_kernel,
        in_specs=[pl.BlockSpec(memory_space=pltpu.SMEM), vmem, vmem] + [vmem] * len(halves),
        out_specs=[vmem, vmem],
        out_shape=[
            jax.ShapeDtypeStruct((query_rows, size), jnp.bfloat16),
            jax.ShapeDtypeStruct((pairs, size), jnp.bfloat16),
        ],
        scratch_shapes=[pltpu.VMEM((pairs, size), jnp.float32)],
        compiler_params=pltpu.CompilerParams(vmem_limit_bytes=8 << 20),
    )(live_count, own, returned, *halves)


def moved_delta(rows, down, up, homes, live_mask):
    slots, features = rows.shape
    replicas = lax.axis_size("replica")
    capacity = max(2, 2 * slots // replicas)
    index = jnp.arange(slots, dtype=jnp.int32)
    earlier = (homes[:, None] == homes[None, :]) & live_mask[None, :] & (index[None, :] < index[:, None])
    position = jnp.sum(earlier.astype(jnp.int32), axis=1)
    target = jnp.where(live_mask, homes * capacity + position, replicas * capacity)
    outgoing = jnp.zeros((replicas * capacity, features), jnp.bfloat16).at[target].set(rows, mode="drop")
    arrived = lax.all_to_all(outgoing, "replica", split_axis=0, concat_axis=0, tiled=True)
    part = jnp.einsum("nd,qd->nq", arrived, down, preferred_element_type=jnp.float32)
    shrunk = lax.psum(part, "tensor").astype(jnp.bfloat16)
    delta = jnp.dot(shrunk, up, preferred_element_type=jnp.float32)
    returned = lax.all_to_all(delta, "replica", split_axis=0, concat_axis=0, tiled=True)
    return jnp.take(returned, target, axis=0, mode="clip")


def home_masks(offsets, adapters, table_ref):
    homes = jnp.zeros(adapters.shape, jnp.int32)
    for adapter in range(table_ref.shape[0]):
        homes = jnp.where(adapters == adapter, table_ref[adapter], homes)
    place = lax.axis_index("replica")
    outer, inner = place // 2, place % 2
    return [homes == (outer ^ offset) * 2 + inner for offset in offsets]


def fill(panel_ref, columns, half, wholes, mine, theirs):
    rank = 2 * half
    start = lax.axis_index("group") * half
    for k, whole in enumerate(wholes):
        panel_ref[pl.ds(k * rank, rank), :] = whole[:, columns] if whole.shape[1] > panel_ref.shape[1] else whole[...]
    for k, (first, second) in enumerate(zip(mine, theirs), len(wholes)):
        panel_ref[pl.ds(pl.multiple_of(k * rank + start, half), half), :] = first[:, columns]
        panel_ref[pl.ds(pl.multiple_of(k * rank + half - start, half), half), :] = second[:, columns]


def rank_kernel(offsets, half, counts, table_ref, rows_ref, other_ref, adapters_ref, other_adapters_ref, *rest):
    wholes, mine, theirs = rest[: counts[0]], rest[counts[0] : sum(counts)], rest[sum(counts) : -2]
    ranks_ref, panel_ref = rest[-2:]
    rank = 2 * half
    slots, features = rows_ref.shape
    fill(panel_ref, slice(0, features), half, wholes, mine, theirs)
    contract = (((1,), (1,)), ((), ()))
    both = jnp.concatenate([rows_ref[...], other_ref[...]], axis=0)
    product = lax.dot_general(panel_ref[...], both, contract, preferred_element_type=jnp.float32)
    for i, adapters in enumerate((adapters_ref, other_adapters_ref)):
        total = jnp.zeros((rank, slots), jnp.float32)
        for k, here in enumerate(home_masks(offsets, adapters[...], table_ref)):
            total += jnp.where(here, product[k * rank : (k + 1) * rank, i * slots : (i + 1) * slots], 0.0)
        ranks_ref[pl.ds(i * rank, rank), :] = total


def delta_of(offsets, at, table_ref, adapters_ref, ranks_ref, got_ref, panel_ref):
    rank = ranks_ref.shape[0] // 2
    shrunk = ranks_ref[pl.ds(at * rank, rank), :] + got_ref[pl.ds(at * rank, rank), :]
    masks = home_masks(offsets, adapters_ref[...], table_ref)
    spread = jnp.concatenate([jnp.where(here, shrunk, 0.0) for here in masks], axis=0).astype(jnp.bfloat16)
    return lax.dot_general(spread, panel_ref[...], (((0,), (0,)), ((), ())), preferred_element_type=jnp.float32)


def sent_kernel(offsets, half, counts, table_ref, adapters_ref, ranks_ref, got_ref, *rest):
    wholes, mine, theirs = rest[: counts[0]], rest[counts[0] : sum(counts)], rest[sum(counts) : -2]
    sent_ref, panel_ref = rest[-2:]
    width = mine[0].shape[1]
    fill(panel_ref, slice(width - sent_ref.shape[1], width), half, wholes, mine, theirs)
    sent_ref[...] = delta_of(offsets, 1, table_ref, adapters_ref, ranks_ref, got_ref, panel_ref).astype(sent_ref.dtype)


def own_kernel(offsets, table_ref, adapters_ref, ranks_ref, got_ref, panel_ref, kept_ref, base_ref, own_ref):
    delta = delta_of(offsets, 0, table_ref, adapters_ref, ranks_ref, got_ref, panel_ref)
    own_ref[...] = delta + (kept_ref[...] + base_ref[...])


def gathered_values(rows, weight, down, up, adapters, table, attention_inputs):
    slots, features = rows.shape
    rank, columns = up.shape
    replicas = lax.axis_size("replica")
    half = rank // 2
    adapters = adapters[None, :]
    vmem = pl.BlockSpec(memory_space=pltpu.VMEM)
    smem = pl.BlockSpec(memory_space=pltpu.SMEM)
    params = pltpu.CompilerParams(vmem_limit_bytes=16 << 20)
    start = lax.axis_index("group") * half
    packed = jnp.concatenate(
        [lax.dynamic_slice_in_dim(down, start, half, 0), lax.dynamic_slice_in_dim(up, start, half, 0)], axis=1
    )
    base_kept, base_sent, rows_near = base_sums(rows, weight)
    other_adapters, sent_rows, base_sent = lax.optimization_barrier((swap(adapters, "replica", 1), rows, base_sent))
    other = swap(sent_rows, "replica", 1)
    near = swap(jnp.concatenate([down, up], axis=1), "replica", 2)
    *attention_arrays, lengths, live_count = attention_inputs
    held = [(0, packed)]
    bit = replicas // 4
    while bit:
        came = [(offset ^ bit, swap(part, "replica", 2 * bit)) for offset, part in held if offset or bit > 1]
        if len(held) == 1:
            first, base_sent = lax.optimization_barrier((came[0][1], base_sent))
            came = [(came[0][0], first)]
        held = held + came
        bit //= 2
    base_got = swap(base_sent, "tensor", 1)
    offsets = [0, 1] + [offset for offset, _ in held[1:]]
    mine = [part for _, part in held[1:]]
    theirs = [swap(part, "group", 1) for part in mine]
    mine[-1], theirs[-2], lengths = lax.optimization_barrier((mine[-1], theirs[-2], lengths))
    halves = cached_attention(0, 2, *attention_arrays, lengths, live_count)

    theirs[-1], halves = lax.optimization_barrier((theirs[-1], halves))
    inputs = [rows_near, other, adapters, other_adapters, down, near] + mine + theirs
    ranks = pl.pallas_call(
        functools.partial(rank_kernel, offsets, half, (2, len(mine))),
        in_specs=[smem] + [vmem] * len(inputs),
        out_specs=vmem,
        out_shape=jax.ShapeDtypeStruct((2 * rank, slots), jnp.float32),
        scratch_shapes=[pltpu.VMEM((len(offsets) * rank, features), jnp.bfloat16)],
        compiler_params=params,
    )(table, *inputs)
    got = swap(ranks, "tensor", 1)
    inputs = [other_adapters, ranks, got, up, near] + mine + theirs
    sent, panel = pl.pallas_call(
        functools.partial(sent_kernel, offsets, half, (2, len(mine))),
        in_specs=[smem] + [vmem] * len(inputs),
        out_specs=[vmem, vmem],
        out_shape=[
            jax.ShapeDtypeStruct((slots, columns), jnp.bfloat16),
            jax.ShapeDtypeStruct((len(offsets) * rank, columns), jnp.bfloat16),
        ],
        compiler_params=params,
    )(table, *inputs)
    returned = swap(sent, "replica", 1)
    inputs = [adapters, ranks, got, panel, base_kept, base_got]
    own = pl.pallas_call(
        functools.partial(own_kernel, offsets),
        in_specs=[smem] + [vmem] * len(inputs),
        out_specs=vmem,
        out_shape=jax.ShapeDtypeStruct((slots, columns), jnp.float32),
        compiler_params=params,
    )(table, *inputs)
    return own, returned, halves


def local(
    hidden,
    queries,
    incoming_keys,
    stored_key_cache,
    stored_value_cache,
    base_value_weight,
    adapter_down_rows,
    adapter_up_rows,
    request_adapter,
    adapter_replica,
    replica_slot_count,
    cache_length,
):
    slots, _, features = hidden.shape
    heads, _, size = stored_key_cache.shape[1:]
    query_heads = queries.shape[3] // size
    replicas = lax.axis_size("replica")
    rows = hidden.reshape(slots, features)
    down, up = adapter_down_rows[0], adapter_up_rows[0]
    query_rows = queries.reshape(slots, heads, query_heads, size).transpose(0, 2, 1, 3).reshape(-1, size)
    attention_inputs = (
        query_rows, incoming_keys, stored_key_cache, stored_value_cache, cache_length, replica_slot_count
    )
    power = replicas >= 8 and replicas & (replicas - 1) == 0
    small = replicas * down.size <= GATHER_BYTES
    if power and small and lax.axis_size("group") == 2:
        own, returned, halves = gathered_values(
            rows, base_value_weight, down, up, request_adapter, adapter_replica, attention_inputs
        )
    else:
        matches = request_adapter[:, None] == jnp.arange(adapter_replica.shape[0], dtype=jnp.int32)[None, :]
        homes = jnp.sum(jnp.where(matches, adapter_replica[None, :], 0), axis=1)
        live_mask = jnp.arange(slots, dtype=jnp.int32) < replica_slot_count[0]
        halves = cached_attention(0, 2, *attention_inputs)
        base_kept, base_sent, _ = base_sums(rows, base_value_weight)
        own, returned = base_kept + swap(base_sent, "tensor", 1), moved_delta(rows, down, up, homes, live_mask)
    attention, fresh_values = finish(own, returned, halves, replica_slot_count)
    attention = attention.reshape(slots, query_heads, heads, size).transpose(0, 2, 1, 3)
    return (
        attention.reshape(slots, 1, heads, query_heads * size),
        fresh_values.reshape(slots, 1, heads, size),
    )


def solution(mesh):
    placed = (
        P(("group", "replica"), None, "tensor"),
        P(("group", "replica"), None, "tensor", None),
        P(("group", "replica"), None, "tensor", None),
        P(("group", "replica"), "tensor", None, None),
        P(("group", "replica"), "tensor", None, None),
        P("tensor", None),
        P("replica", None, "tensor"),
        P("replica", None, "tensor"),
        P("replica"),
        P(),
        P("replica"),
        P("replica"),
    )
    return jax.shard_map(
        local,
        mesh=mesh,
        in_specs=placed,
        out_specs=(
            P(("group", "replica"), None, "tensor", None),
            P(("group", "replica"), None, "tensor", None),
        ),
        check_vma=False,
    )
```
